256 devices in a mesh: replica: 8 (over z), dp: 8 (over x_lo, y), section: 4 (over x_hi, core).
Axes of the slice: x: 4 (x_hi: 2, x_lo: 2; x = x_hi * 2 + x_lo), y: 4, z: 8, core: 2. Of those that a mesh axis runs over, the one named last changes fastest.
Arguments:
- activations: bfloat16 [8, 4, 3072, 4096], P('replica', 'section', 'dp'), may hold values from -0.4375 to 0.4375
- key_cotangent: bfloat16 [8, 4, 3072, 1024], P('replica', 'section', 'dp'), may hold values from -6 to 6
- key_weight: bfloat16 [8, 4, 4096, 1024], P('replica', 'section', 'dp'), may hold values from -0.09375 to 0.09375
- delta_codes: bfloat16 [8, 4, 4096, 1024], P('replica', 'section', 'dp'), may hold values from -127 to 127, as said below
- delta_exponents: int32 [8, 4, 4096, 8], P('replica', 'section', 'dp'), may hold values from -10 to -6
- outer_momentum: float32 [4, 4096, 1024], P('section', ('dp', 'replica')), may hold values from -6 to 6
- outer_master: float32 [4, 4096, 1024], P('section', ('dp', 'replica')), may hold values from -6 to 6
Outputs:
- sent_cotangent: bfloat16 [8, 4, 3072, 4096], P('replica', 'section', 'dp')
- weight_grad: bfloat16 [8, 4, 4096, 1024], P('replica', 'section', 'dp')
- momentum_new: float32 [4, 4096, 1024], P('section', ('dp', 'replica'))
- master_new: float32 [4, 4096, 1024], P('section', ('dp', 'replica'))
- synced_weight: bfloat16 [4, 4096, 1024], P('section', 'dp')
The draws below stay inside these ranges and needn't reach their ends.
Inputs may be any that keep to these rules, and one draw needn't show every extreme that they name: delta_codes holds whole numbers.
All inputs are finite; a program needn't handle non-finite values.
Results may differ from the reference program's by a relative error of at most 0.017.
Values may be sent and summed in bfloat16 or wider, within the bound.
No kernel may reach another device: no remote copies, remote signals or barrier semaphores. Data moves between devices by JAX's collectives and lax.ppermute only.
A program may use at most 128 MiB of HBM per device.

```python
import jax
import jax.numpy as jnp
from jax import lax

D = 4096
KV = 1024
EB = 128
TOK_DEV = 384
TOKENS = 3072
LAYERS = 4
N_REPLICA = 8
N_DP = 8


def draw_delta_codes(key, part):
    key = jax.random.fold_in(key, 11)
    values = jax.random.randint(key, (N_REPLICA, LAYERS, D, KV), -127, 128)
    return values.astype(jnp.float32).astype(jnp.bfloat16)


def with_ends(values, own_key, low, high):
    spot = [jax.random.randint(jax.random.fold_in(own_key, axis), (), 0, length) for axis, length in enumerate(values.shape)]
    longest = values.shape.index(max(values.shape))
    neighbour = spot[:longest] + [(spot[longest] + 1) % values.shape[longest]] + spot[longest + 1:]
    return values.at[tuple(spot)].set(low).at[tuple(neighbour)].set(high)


def strengthened(entries, stream_key, source, target, blocks, factor):
    def block_of(dim):
        return (jnp.arange(entries.shape[dim]) // (entries.shape[dim] // blocks)).reshape((-1,) + (1,) * (entries.ndim - 1 - dim))

    first = jax.random.permutation(stream_key, blocks)[block_of(target)]
    second = (block_of(target) + blocks // 2) % blocks
    return jnp.where((block_of(source) == first) | (block_of(source) == second), factor * entries, entries)


def levels(rng, extent, shards, least, largest):
    def one(position, shards_of):
        heights = jax.random.uniform(jax.random.fold_in(jax.random.fold_in(rng, 6), position), (shards_of,), jnp.float32, least / len(shards), largest / len(shards))
        return jnp.repeat(jnp.exp(heights), extent[position] // shards_of).reshape((-1,) + (1,) * (len(extent) - position - 1))

    gain = one(*shards[0])
    for cut in shards[1:]:
        gain = gain * one(*cut)
    return gain


def bell_draw(stream_key, shape, spread, reach, pieces=(), dtype=jnp.bfloat16):
    factor_of = levels(stream_key, shape, pieces, -0.22, 0.18) if pieces else 1.0
    entries = jax.random.normal(stream_key, shape, jnp.float32) * spread * factor_of
    return jnp.minimum(jnp.maximum(entries, -reach), reach).astype(dtype)


def heavy_noise(rng, extent, width, bound, cuts, heavy, held_as=jnp.bfloat16):
    values = width * jax.random.normal(rng, extent, jnp.float32)
    if cuts:
        values = values * levels(rng, extent, cuts, -0.22, 0.18)
    return jnp.clip(strengthened(values, jax.random.fold_in(rng, 3), *heavy), -bound, bound).astype(held_as)


def setup_inputs(seed: int = 0) -> dict:
    key_of = jax.random.split(jax.random.key(seed), 8)
    activations = heavy_noise(key_of[0], (N_REPLICA, LAYERS, TOKENS, D), 0.02, 0.4375, ((0, 8), (1, 4), (2, 8)), (2, 3, 8, 2.0))
    key_cotangent = bell_draw(key_of[1], (N_REPLICA, LAYERS, TOKENS, KV), 1.0, 6.0, ((0, 8), (1, 4), (2, 8)))
    key_weight = bell_draw(key_of[2], (N_REPLICA, LAYERS, D, KV), D ** -0.5, 0.09375, ((0, 8), (1, 4), (2, 8)))
    delta_codes = draw_delta_codes(jax.random.fold_in(key_of[7], 71), 0)
    delta_exponents = with_ends(jax.random.randint(key_of[4], (N_REPLICA, LAYERS, D, KV // EB), -10, -5), jax.random.fold_in(key_of[4], 1), -10, (-5) - 1).astype(jnp.int32)
    outer_momentum = bell_draw(key_of[5], (LAYERS, D, KV), 0.5, 6.0, ((0, 4), (1, 64)), jnp.float32)
    outer_master = bell_draw(key_of[6], (LAYERS, D, KV), 0.5, 6.0, ((0, 4), (1, 64)), jnp.float32)
    return dict(activations=activations, key_cotangent=key_cotangent, key_weight=key_weight, delta_codes=delta_codes, delta_exponents=delta_exponents, outer_momentum=outer_momentum, outer_master=outer_master)


def one_layer(features, cotang, weights):
    input_grad = lax.dot_general(cotang, weights, (((1,), (1,)), ((), ())), preferred_element_type=jnp.float32).astype(jnp.bfloat16)
    blocks_x = features.reshape(N_DP, TOK_DEV, D)
    blocks_k = cotang.reshape(N_DP, TOK_DEV, KV)

    def accumulate(total, pair):
        part_x, part_k = pair
        partial_value = lax.dot_general(part_x, part_k, (((0,), (0,)), ((), ())), preferred_element_type=jnp.float32).astype(jnp.bfloat16)
        return total + partial_value.astype(jnp.float32), 0

    total, unused = lax.scan(accumulate, jnp.zeros((D, KV), jnp.float32), (blocks_x, blocks_k))
    return input_grad, total.astype(jnp.bfloat16)


def reference(activations, key_cotangent, key_weight, delta_codes, delta_exponents, outer_momentum, outer_master):
    count = N_REPLICA * LAYERS
    flat_x = activations.reshape(count, TOKENS, D)
    flat_k = key_cotangent.reshape(count, TOKENS, KV)
    flat_w = key_weight.reshape(count, D, KV)
    input_grad, weight_grad = lax.map(lambda trio: one_layer(trio[0], trio[1], trio[2]), (flat_x, flat_k, flat_w))
    input_grad = input_grad.reshape(N_REPLICA, LAYERS, TOKENS, D)
    weight_grad = weight_grad.reshape(N_REPLICA, LAYERS, D, KV)
    sent_cotangent = jnp.concatenate([input_grad[:, 1:], jnp.zeros_like(input_grad[:, :1])], axis=1)
    scales = jnp.exp2(delta_exponents.astype(jnp.float32))
    delta = delta_codes.astype(jnp.float32).reshape(N_REPLICA, LAYERS, D, KV // EB, EB) * scales[..., None]
    delta = delta.reshape(N_REPLICA, LAYERS, D, KV)
    mean_delta = jnp.sum(delta, axis=0) / N_REPLICA
    momentum_new = 0.9 * outer_momentum + mean_delta
    master_new = outer_master - 0.7 * (mean_delta + 0.9 * momentum_new)
    synced_weight = master_new.astype(jnp.bfloat16)
    return sent_cotangent, weight_grad, momentum_new, master_new, synced_weight
```

```python
import jax
import jax.numpy as jnp
from jax import lax
from jax.sharding import PartitionSpec as P

NX, NY = 2, 4


def solution(mesh):
    sections = mesh.shape["section"]
    replicas = mesh.shape["replica"]

    def moved(value, to, first=0):
        pairs = []
        for x in range(NX):
            for y in range(NY):
                for s in range(first, sections):
                    tx, ty, ts = to(x, y, s)
                    if 0 <= ts < sections:
                        source = (x * NY + y) * sections + s
                        target = (tx % NX * NY + ty % NY) * sections + ts
                        pairs.append((source, target))
        return lax.ppermute(value, ("dp", "section"), pairs)

    def body(act, cot, w, codes, exps, mom, mas):
        act, cot, w, codes, exps, mom, mas = (
            act[0, 0], cot[0, 0], w[0, 0], codes[0, 0], exps[0, 0], mom[0], mas[0])
        rows, width = w.shape
        half = NY * rows
        tok = act.shape[0]
        dp = lax.axis_index("dp")
        x, y = dp // NY, dp % NY

        with jax.named_scope("pair_swap"):
            cot_o = moved(cot, lambda x, y, s: (x + 1, y, s))
            act_o = moved(
                lax.dynamic_slice(act, (0, (1 - x) * half), (tok, half)),
                lambda x, y, s: (x + 1, y, s))
        with jax.named_scope("gather_weight"):
            ws = [w] + [moved(w, lambda x, y, s, r=r: (x, y - r, s), 1) for r in (1, 2, 3)]

        with jax.named_scope("outer"):
            scales = jnp.exp2(exps.astype(jnp.float32))
            blocks = scales.shape[1]
            delta = codes.astype(jnp.float32).reshape(rows, blocks, width // blocks) * scales[..., None]
            delta = delta.reshape(replicas, rows // replicas, width).astype(jnp.bfloat16)
            delta = lax.all_to_all(delta, "replica", 0, 0)
            mean = jnp.sum(delta.astype(jnp.float32), axis=0) / replicas
            mom_new = 0.9 * mom + mean
            mas_new = mas - 0.7 * (mean + 0.9 * mom_new)
            synced = lax.all_gather(mas_new.astype(jnp.bfloat16), "replica", axis=0, tiled=True)

        with jax.named_scope("input_grad"):
            def grads(c):
                return jnp.stack([lax.dot_general(
                    c, b, (((1,), (1,)), ((), ())), preferred_element_type=jnp.float32
                ).astype(jnp.bfloat16) for b in ws])
            other = moved(grads(cot_o), lambda x, y, s: (x + 1, y, s - 1), 1)
            own = moved(grads(cot), lambda x, y, s: (x, y, s - 1), 1)

        with jax.named_scope("weight_grad"):
            own_half = lax.dynamic_slice(act, (0, x * half), (tok, half))
            pair_act = jnp.concatenate([own_half, act_o], 0)
            pair_cot = jnp.concatenate([cot, cot_o], 0)
            parts = []
            for r in (2, 1, 3, 0):
                block = lax.dynamic_slice(pair_act, (0, (y + r) % NY * rows), (2 * tok, rows))
                parts.append(lax.dot_general(
                    block, pair_cot, (((0,), (0,)), ((), ())), preferred_element_type=jnp.float32))
            grad = parts[3]
            for r, part in zip((2, 1, 3), parts):
                grad = grad + moved(
                    part.astype(jnp.bfloat16), lambda x, y, s, r=r: (x, y + r, s)).astype(jnp.float32)
            grad = grad.astype(jnp.bfloat16)

        with jax.named_scope("assemble"):
            def placed(blocks):
                flat = jnp.concatenate([blocks, blocks], 0)
                flat = lax.dynamic_slice(flat, ((NY - y) % NY, 0, 0), blocks.shape)
                return jnp.concatenate(list(flat), 1)
            own, other = placed(own), placed(other)
            sent = jnp.where(x == 0, jnp.concatenate([own, other], 1), jnp.concatenate([other, own], 1))
        return (sent[None, None], grad[None, None], mom_new[None], mas_new[None], synced[None])

    placed = (
        P("replica", "section", "dp", None),
        P("replica", "section", "dp", None),
        P("replica", "section", "dp", None),
        P("replica", "section", "dp", None),
        P("replica", "section", "dp", None),
        P("section", ("dp", "replica"), None),
        P("section", ("dp", "replica"), None),
    )
    return jax.shard_map(
        body,
        mesh=mesh,
        in_specs=placed,
        out_specs=(
            P("replica", "section", "dp", None),
            P("replica", "section", "dp", None),
            P("section", ("dp", "replica"), None),
            P("section", ("dp", "replica"), None),
            P("section", "dp", None),
        ),
        check_vma=False,
    )
```

```python
import jax
import jax.numpy as jnp
from jax import lax
from jax.experimental import pallas as pl
from jax.experimental.pallas import tpu as pltpu
from jax.sharding import PartitionSpec as P

NX, NY = 2, 4
BF16, F32 = jnp.bfloat16, jnp.float32
PARAMS = pltpu.CompilerParams(vmem_limit_bytes=48 * 1024 * 1024)


def call(kernel, name, grid, in_specs, out_specs, out_shape, aliases=None, after=()):
    inputs, count = len(in_specs), len(after)

    def with_after(pos, *refs):
        kernel(pos, *refs[:inputs], *refs[inputs + count:])

    run = pl.pallas_call(
        with_after,
        grid_spec=pltpu.PrefetchScalarGridSpec(
            num_scalar_prefetch=1, grid=grid, in_specs=list(in_specs) + [pl.BlockSpec(memory_space=pl.ANY)] * count,
            out_specs=out_specs),
        out_shape=out_shape,
        input_output_aliases=aliases or {},
        compiler_params=PARAMS,
        cost_estimate=pl.CostEstimate(flops=1, bytes_accessed=1, transcendentals=0),
        name=name,
    )
    return lambda *operands: run(*operands, *after)


def block_of(pos, r):
    return lax.rem(pos[1] + r, NY)


def scaled(codes_ref, exps_ref, out_ref):
    scales = jnp.exp2(exps_ref[...].astype(F32))
    blocks = scales.shape[1]
    wide = codes_ref.shape[1] // blocks
    for b in range(blocks):
        cols = slice(b * wide, (b + 1) * wide)
        out_ref[:, cols] = (codes_ref[:, cols].astype(F32) * scales[:, b:b + 1]).astype(BF16)


def delta_kernel(pos, codes_keep, codes_send, exps_keep, exps_send, keep_ref, send_ref):
    scaled(codes_keep, exps_keep, keep_ref)
    scaled(codes_send, exps_send, send_ref)


def add_kernel(pos, keep, arrived, out_ref):
    out_ref[...] = (keep[...].astype(F32) + arrived[...].astype(F32)).astype(BF16)


def input_grad(c_ref, c_o_ref, w_ref):
    both = jnp.concatenate([c_ref[...], c_o_ref[...]], 0)
    out = lax.dot_general(
        both, w_ref[...], (((1,), (1,)), ((), ())), preferred_element_type=F32).astype(BF16)
    return out[:c_ref.shape[0]], out[c_ref.shape[0]:]


def input_grad_kernel(pos, c_ref, c_o_ref, *refs):
    *w_refs, own_ref, other_ref = refs
    for i, w_ref in enumerate(w_refs):
        @pl.when(pl.program_id(0) == i)
        def _():
            own_ref[...], other_ref[...] = input_grad(c_ref, c_o_ref, w_ref)


def far_input_grad_kernel(pos, c_ref, c_o_ref, up_ref, down_ref, own_ref, other_ref):
    half = up_ref.shape[0]
    own_ref[:, :half], other_ref[:, :half] = input_grad(c_ref, c_o_ref, up_ref)
    own_ref[:, half:], other_ref[:, half:] = input_grad(c_ref, c_o_ref, down_ref)


def partial_grad(a_ref, a_o_ref, c_ref, c_o_ref):
    dims = (((0,), (0,)), ((), ()))
    return lax.dot_general(a_ref[...], c_ref[...], dims, preferred_element_type=F32) + lax.dot_general(
        a_o_ref[...], c_o_ref[...], dims, preferred_element_type=F32)


def far_grad_kernel(pos, a_ref, a_o_ref, c_ref, c_o_ref, w_up, w_down, up_ref, down_ref):
    total = partial_grad(a_ref, a_o_ref, c_ref, c_o_ref).astype(BF16)
    half = total.shape[0] // 2
    up_ref[:half] = total[:half]
    up_ref[half:] = w_up[...]
    down_ref[:half] = total[half:]
    down_ref[half:] = w_down[...]


def near_grad_kernel(upper, pos, a_ref, a_o_ref, c_ref, c_o_ref, arrived, out_ref):
    total = partial_grad(a_ref, a_o_ref, c_ref, c_o_ref)
    half = arrived.shape[0]
    first, second = total[:half], total[half:]
    if upper:
        first = first + arrived[...].astype(F32)
    else:
        second = second + arrived[...].astype(F32)
    out_ref[:half] = first.astype(BF16)
    out_ref[half:] = second.astype(BF16)


def last_grad_kernel(pos, a_ref, a_o_ref, c_ref, c_o_ref, p1, p3, out_ref):
    total = partial_grad(a_ref, a_o_ref, c_ref, c_o_ref)
    total = total + p1[...].astype(F32) + p3[...].astype(F32)
    out_ref[...] = total.astype(BF16)


def outer_kernel(pos, d_ref, mom_ref, mas_ref, mom_out, mas_out, sync_out):
    count = d_ref.shape[0]
    total = d_ref[0].astype(F32)
    for i in range(1, count):
        total = total + d_ref[i].astype(F32)
    mean = total / (2 * count)
    mom = 0.9 * mom_ref[...] + mean
    mas = mas_ref[...] - 0.7 * (mean + 0.9 * mom)
    mom_out[...] = mom
    mas_out[...] = mas
    synced = mas.astype(BF16)
    for i in range(sync_out.shape[0]):
        sync_out[i] = synced


def place_kernel(pos, most, rest, *refs):
    step = pl.program_id(0)
    out_ref = refs[-1]

    @pl.when(step < NY - 1)
    def _():
        out_ref[...] = most[...]

    @pl.when(step == NY - 1)
    def _():
        out_ref[...] = rest[...]


def copy_kernel(pos, part_ref, *refs):
    refs[-1][...] = part_ref[...]


def solution(mesh):
    sections = mesh.shape["section"]
    replicas = mesh.shape["replica"]

    def moved(value, to, first=0):
        pairs = []
        for x in range(NX):
            for y in range(NY):
                for s in range(first, sections):
                    tx, ty, ts = to(x, y, s)
                    if 0 <= ts < sections:
                        source = (x * NY + y) * sections + s
                        target = (tx % NX * NY + ty % NY) * sections + ts
                        pairs.append((source, target))
        return lax.ppermute(value, ("dp", "section"), pairs)

    def body(act, cot, w, codes, exps, mom, mas):
        act, cot, w, codes, exps, mom, mas = (
            act[0, 0], cot[0, 0], w[0, 0], codes[0, 0], exps[0, 0], mom[0], mas[0])
        rows, width = w.shape
        tok = act.shape[0]
        dp = lax.axis_index("dp")
        pos = jnp.stack([dp // NY, dp % NY, lax.axis_index("replica") % 2]).astype(jnp.int32)
        whole = lambda shape: pl.BlockSpec(shape, lambda *_: (0,) * len(shape))
        share, half = rows // replicas, rows // 2
        up = lambda x, y, s: (x, y + 1, s)
        down = lambda x, y, s: (x, y - 1, s)
        swap = lambda x, y, s: (x + 1, y, s)

        def swapped_blocks(rs, after):
            number, count = rs
            at = lambda i, pos: (0, (1 - pos[0]) * NY + block_of(pos, number(i)))
            send = call(
                copy_kernel, "split", (count,), [pl.BlockSpec((tok, rows), at)],
                pl.BlockSpec((tok, rows), lambda i, pos: (0, i)),
                jax.ShapeDtypeStruct((tok, count * rows), BF16), after=after,
            )(pos, act)
            return send, moved(send, swap)

        def part_rows(n, m):
            return pl.BlockSpec((n, m), lambda i, pos: (i, 0))

        def part_of(shape, i, j):
            return pl.BlockSpec(shape, lambda *_: (i, j))

        def blocks(r, part):
            return [pl.BlockSpec((tok, rows), lambda _, pos: (0, pos[0] * NY + block_of(pos, r))),
                    part_of((tok, rows), 0, part), whole((tok, width)), whole((tok, width))]

        def near(r, part, arrived, after):
            part = call(
                lambda *refs: near_grad_kernel(r == 1, *refs), "near_grad", (1,),
                blocks(r, part) + [part_of((half, width), 0, 0)], whole((rows, width)),
                jax.ShapeDtypeStruct((rows, width), BF16), after=after,
            )(pos, act, act_o, cot, cot_o, arrived)
            return part, moved(part, up if r == 1 else down)

        def place(most, rest, flip, after, base=None):
            number = lambda i: i + i // 2 - i // 3 * 2
            at = lambda i, pos: (0, (1 - pos[0] if flip else pos[0]) * NY + block_of(pos, number(i)))
            return call(
                place_kernel, "place", (NY,),
                [pl.BlockSpec((tok, rows), lambda i, pos: (0, jnp.minimum(i, NY - 2))), whole((tok, rows))]
                + ([pl.BlockSpec(memory_space=pl.ANY)] if base is not None else []),
                pl.BlockSpec((tok, rows), at), jax.ShapeDtypeStruct(act.shape, BF16),
                {3: 0} if base is not None else None, after=after,
            )(pos, most, rest, *([base] if base is not None else []))

        with jax.named_scope("pair_swap"):
            send, act_2 = swapped_blocks((lambda i: 2, 1), [])
            cot_o = moved(cot, swap)
        with jax.named_scope("gather_weight"):
            w_3 = moved(w, up)
            w_1 = moved(w, down)
        with jax.named_scope("delta"):
            row = lambda n, other: pl.BlockSpec(
                (share, n), lambda i, pos: (2 * i + (1 - pos[2] if other else pos[2]), 0))
            out = pl.BlockSpec((share, width), lambda i, pos: (i, 0))
            n_exp = exps.shape[1]
            keep, send = call(
                delta_kernel, "delta", (replicas // 2,),
                [row(width, False), row(width, True), row(n_exp, False), row(n_exp, True)],
                [out, out], [jax.ShapeDtypeStruct((rows // 2, width), BF16)] * 2, after=[send],
            )(pos, codes, codes, exps, exps)
            arrived = lax.ppermute(send, "replica", [(i, i ^ 1) for i in range(replicas)])
            pair_sum = call(
                add_kernel, "add", (2,), [part_rows(half // 2, width)] * 2, part_rows(half // 2, width),
                jax.ShapeDtypeStruct((half, width), BF16), after=[w_3, w_1, cot_o],
            )(pos, keep, arrived)
            deltas = lax.all_to_all(
                pair_sum.reshape(replicas // 2, share, width), "replica", 0, 0,
                axis_index_groups=[list(range(k, replicas, 2)) for k in range(2)])
        with jax.named_scope("far"):
            far_up, far_down = call(
                far_grad_kernel, "far_grad", (1,),
                blocks(2, 0) + [part_of((half, width), 0, 0), part_of((half, width), 1, 0)],
                [whole((rows, width))] * 2, [jax.ShapeDtypeStruct((rows, width), BF16)] * 2, after=[pair_sum],
            )(pos, act, act_2, cot, cot_o, w_3, w_1)
            up_o = moved(far_up, up)
            down_o = moved(far_down, down)
        with jax.named_scope("pair_swap"):
            send, act_o = swapped_blocks((lambda i: 2 * i + 1 - 5 * (i // 2), 3), [far_up])
        with jax.named_scope("input_grad"):
            shift = lambda x, y, s: (x, y, s - 1)
            flip = lambda x, y, s: (x + 1, y, s - 1)
            out = pl.BlockSpec((tok, rows), lambda i, pos: (0, i))
            own, other = call(
                input_grad_kernel, "input_grad", (NY - 1,),
                [whole((tok, width))] * 2 + [whole((rows, width))] * 3, [out, out],
                [jax.ShapeDtypeStruct((tok, (NY - 1) * rows), BF16)] * 2, after=[send],
            )(pos, cot, cot_o, w, w_1, w_3)
            sent_other, sent_own = moved(other, flip, 1), moved(own, shift, 1)
        with jax.named_scope("outer"):
            cols = width // 2
            wide = pl.BlockSpec((replicas, share, cols), lambda i, pos: (0, 0, i))
            some = pl.BlockSpec((replicas // 2, share, cols), lambda i, pos: (0, 0, i))
            thin = pl.BlockSpec((share, cols), lambda i, pos: (0, i))
            mom_new, mas_new, to_sync = call(
                outer_kernel, "outer", (2,), [some, thin, thin], [thin, thin, wide],
                [jax.ShapeDtypeStruct(mom.shape, F32)] * 2
                + [jax.ShapeDtypeStruct((replicas, share, width), BF16)], after=[own],
            )(pos, deltas, mom, mas)
            synced = lax.all_to_all(to_sync, "replica", 0, 0).reshape(rows, width)
        with jax.named_scope("weight_grad"):
            part, near_1 = near(1, 0, up_o, [to_sync])
            part, near_3 = near(3, 1, down_o, [part])
        with jax.named_scope("input_grad"):
            own, other = call(
                far_input_grad_kernel, "far_input_grad", (1,),
                [whole((tok, width))] * 2 + [part_of((half, width), 1, 0)] * 2, [whole((tok, rows))] * 2,
                [jax.ShapeDtypeStruct((tok, rows), BF16)] * 2, after=[part],
            )(pos, cot, cot_o, up_o, down_o)
            sent_other_2, sent_own_2 = moved(other, flip, 1), moved(own, shift, 1)
        with jax.named_scope("assemble"):
            sent = place(sent_own, sent_own_2, False, [own])
            sent = place(sent_other, sent_other_2, True, [], sent)
        with jax.named_scope("weight_grad"):
            grad = call(
                last_grad_kernel, "last_grad", (1,), blocks(0, 2) + [whole((rows, width))] * 2,
                whole((rows, width)), jax.ShapeDtypeStruct((rows, width), BF16), after=[sent],
            )(pos, act, act_o, cot, cot_o, near_1, near_3)
        return (sent[None, None], grad[None, None], mom_new[None], mas_new[None], synced[None])

    placed = (
        P("replica", "section", "dp", None),
        P("replica", "section", "dp", None),
        P("replica", "section", "dp", None),
        P("replica", "section", "dp", None),
        P("replica", "section", "dp", None),
        P("section", ("dp", "replica"), None),
        P("section", ("dp", "replica"), None),
    )
    return jax.shard_map(
        body,
        mesh=mesh,
        in_specs=placed,
        out_specs=(
            P("replica", "section", "dp", None),
            P("replica", "section", "dp", None),
            P("section", ("dp", "replica"), None),
            P("section", ("dp", "replica"), None),
            P("section", "dp", None),
        ),
        check_vma=False,
    )
```

```python
import jax
import jax.numpy as jnp
from jax import lax
from jax.experimental import pallas as pl
from jax.experimental.pallas import tpu as pltpu
from jax.sharding import PartitionSpec as P

NX, NY = 2, 4
BF16, F32 = jnp.bfloat16, jnp.float32
PARAMS = pltpu.CompilerParams(vmem_limit_bytes=48 * 1024 * 1024)


def call(kernel, name, grid, in_specs, out_specs, out_shape, aliases=None, after=(), sems=0):
    inputs, count = len(in_specs), len(after)

    def with_after(pos, *refs):
        kernel(pos, *refs[:inputs], *refs[inputs + count:])

    run = pl.pallas_call(
        with_after,
        grid_spec=pltpu.PrefetchScalarGridSpec(
            num_scalar_prefetch=1, grid=grid, in_specs=list(in_specs) + [pl.BlockSpec(memory_space=pl.ANY)] * count,
            out_specs=out_specs, scratch_shapes=[pltpu.SemaphoreType.DMA((sems,))] if sems else []),
        out_shape=out_shape,
        input_output_aliases=aliases or {},
        compiler_params=PARAMS,
        cost_estimate=pl.CostEstimate(flops=1, bytes_accessed=1, transcendentals=0),
        name=name,
    )
    return lambda *operands: run(*operands, *after)


def block_of(pos, r):
    return lax.rem(pos[1] + r, NY)


def scaled(codes_ref, exps_ref, out_ref):
    scales = jnp.exp2(exps_ref[...].astype(F32))
    blocks = scales.shape[1]
    wide = codes_ref.shape[1] // blocks
    for b in range(blocks):
        cols = slice(b * wide, (b + 1) * wide)
        out_ref[:, cols] = (codes_ref[:, cols].astype(F32) * scales[:, b:b + 1]).astype(BF16)


def delta_kernel(pos, codes_keep, codes_send, exps_keep, exps_send, keep_ref, send_ref):
    scaled(codes_keep, exps_keep, keep_ref)
    scaled(codes_send, exps_send, send_ref)


def add_kernel(pos, keep, arrived, out_ref):
    out_ref[...] = (keep[...].astype(F32) + arrived[...].astype(F32)).astype(BF16)


def input_grad(c_ref, c_o_ref, w_ref):
    both = jnp.concatenate([c_ref[...], c_o_ref[...]], 0)
    out = lax.dot_general(
        both, w_ref[...], (((1,), (1,)), ((), ())), preferred_element_type=F32).astype(BF16)
    return out[:c_ref.shape[0]], out[c_ref.shape[0]:]


def input_grad_kernel(pos, c_ref, c_o_ref, *refs):
    *w_refs, own_ref, other_ref = refs
    for i, w_ref in enumerate(w_refs):
        @pl.when(pl.program_id(0) == i)
        def _():
            own_ref[...], other_ref[...] = input_grad(c_ref, c_o_ref, w_ref)


def far_input_grad_kernel(pos, c_ref, c_o_ref, up_ref, down_ref, own_ref, other_ref):
    half = up_ref.shape[0]
    own_ref[:, :half], other_ref[:, :half] = input_grad(c_ref, c_o_ref, up_ref)
    own_ref[:, half:], other_ref[:, half:] = input_grad(c_ref, c_o_ref, down_ref)


def partial_grad(a_ref, a_o_ref, c_ref, c_o_ref):
    dims = (((0,), (0,)), ((), ()))
    return lax.dot_general(a_ref[...], c_ref[...], dims, preferred_element_type=F32) + lax.dot_general(
        a_o_ref[...], c_o_ref[...], dims, preferred_element_type=F32)


def far_grad_kernel(pos, a_ref, a_o_ref, c_ref, c_o_ref, w_up, w_down, up_ref, down_ref):
    total = partial_grad(a_ref, a_o_ref, c_ref, c_o_ref).astype(BF16)
    half = total.shape[0] // 2
    up_ref[:half] = total[:half]
    up_ref[half:] = w_up[...]
    down_ref[:half] = total[half:]
    down_ref[half:] = w_down[...]


def near_grad_kernel(upper, pos, a_ref, a_o_ref, c_ref, c_o_ref, arrived, out_ref):
    total = partial_grad(a_ref, a_o_ref, c_ref, c_o_ref)
    half = arrived.shape[0]
    first, second = total[:half], total[half:]
    if upper:
        first = first + arrived[...].astype(F32)
    else:
        second = second + arrived[...].astype(F32)
    out_ref[:half] = first.astype(BF16)
    out_ref[half:] = second.astype(BF16)


def last_grad_kernel(pos, a_ref, a_o_ref, c_ref, c_o_ref, p1, p3, out_ref):
    total = partial_grad(a_ref, a_o_ref, c_ref, c_o_ref)
    total = total + p1[...].astype(F32) + p3[...].astype(F32)
    out_ref[...] = total.astype(BF16)


def outer_kernel(pos, d_ref, mom_ref, mas_ref, mom_out, mas_out, sync_out):
    count = d_ref.shape[0]
    total = d_ref[0].astype(F32)
    for i in range(1, count):
        total = total + d_ref[i].astype(F32)
    mean = total / (2 * count)
    mom = 0.9 * mom_ref[...] + mean
    mas = mas_ref[...] - 0.7 * (mean + 0.9 * mom)
    mom_out[...] = mom
    mas_out[...] = mas
    synced = mas.astype(BF16)
    for i in range(sync_out.shape[0]):
        sync_out[i] = synced


def place_kernel(pos, most, rest, *refs):
    step = pl.program_id(0)
    out_ref = refs[-1]

    @pl.when(step < NY - 1)
    def _():
        out_ref[...] = most[...]

    @pl.when(step == NY - 1)
    def _():
        out_ref[...] = rest[...]


def split_kernel(rows, numbers, pos, a_ref, out_ref, sems):
    first = (1 - pos[0]) * NY
    moves = []
    for k, r in enumerate(numbers):
        at = pl.multiple_of((first + block_of(pos, r)) * rows, rows)
        moves.append(pltpu.make_async_copy(
            a_ref.at[:, pl.ds(at, rows)], out_ref.at[:, pl.ds(k * rows, rows)], sems.at[k]))
    for move in moves:
        move.start()
    for move in moves:
        move.wait()


def copy_kernel(pos, part_ref, *refs):
    refs[-1][...] = part_ref[...]


def solution(mesh):
    sections = mesh.shape["section"]
    replicas = mesh.shape["replica"]

    def moved(value, to, first=0):
        pairs = []
        for x in range(NX):
            for y in range(NY):
                for s in range(first, sections):
                    tx, ty, ts = to(x, y, s)
                    if 0 <= ts < sections:
                        source = (x * NY + y) * sections + s
                        target = (tx % NX * NY + ty % NY) * sections + ts
                        pairs.append((source, target))
        return lax.ppermute(value, ("dp", "section"), pairs)

    def body(act, cot, w, codes, exps, mom, mas):
        act, cot, w, codes, exps, mom, mas = (
            act[0, 0], cot[0, 0], w[0, 0], codes[0, 0], exps[0, 0], mom[0], mas[0])
        rows, width = w.shape
        tok = act.shape[0]
        dp = lax.axis_index("dp")
        pos = jnp.stack([dp // NY, dp % NY, lax.axis_index("replica") % 2]).astype(jnp.int32)
        whole = lambda shape: pl.BlockSpec(shape, lambda *_: (0,) * len(shape))
        share, half = rows // replicas, rows // 2
        up = lambda x, y, s: (x, y + 1, s)
        down = lambda x, y, s: (x, y - 1, s)
        swap = lambda x, y, s: (x + 1, y, s)

        def swapped_blocks(rs, after):
            number, count = rs
            at = lambda i, pos: (0, (1 - pos[0]) * NY + block_of(pos, number(i)))
            send = call(
                copy_kernel, "split", (count,), [pl.BlockSpec((tok, rows), at)],
                pl.BlockSpec((tok, rows), lambda i, pos: (0, i)),
                jax.ShapeDtypeStruct((tok, count * rows), BF16), after=after,
            )(pos, act)
            return send, moved(send, swap)

        def part_rows(n, m):
            return pl.BlockSpec((n, m), lambda i, pos: (i, 0))

        def part_of(shape, i, j):
            return pl.BlockSpec(shape, lambda *_: (i, j))

        def blocks(r, part):
            return [pl.BlockSpec((tok, rows), lambda _, pos: (0, pos[0] * NY + block_of(pos, r))),
                    part_of((tok, rows), 0, part), whole((tok, width)), whole((tok, width))]

        def near(r, part, arrived, after):
            part = call(
                lambda *refs: near_grad_kernel(r == 1, *refs), "near_grad", (1,),
                blocks(r, part) + [part_of((half, width), 0, 0)], whole((rows, width)),
                jax.ShapeDtypeStruct((rows, width), BF16), after=after,
            )(pos, act, act_o, cot, cot_o, arrived)
            return part, moved(part, up if r == 1 else down)

        def place(most, rest, flip, after, base=None):
            number = lambda i: i + i // 2 - i // 3 * 2
            at = lambda i, pos: (0, (1 - pos[0] if flip else pos[0]) * NY + block_of(pos, number(i)))
            return call(
                place_kernel, "place", (NY,),
                [pl.BlockSpec((tok, rows), lambda i, pos: (0, jnp.minimum(i, NY - 2))), whole((tok, rows))]
                + ([pl.BlockSpec(memory_space=pl.ANY)] if base is not None else []),
                pl.BlockSpec((tok, rows), at), jax.ShapeDtypeStruct(act.shape, BF16),
                {3: 0} if base is not None else None, after=after,
            )(pos, most, rest, *([base] if base is not None else []))

        with jax.named_scope("pair_swap"):
            send, act_2 = swapped_blocks((lambda i: 2, 1), [])
            cot_o = moved(cot, swap)
        with jax.named_scope("gather_weight"):
            w_3 = moved(w, up)
            w_1 = moved(w, down)
        with jax.named_scope("delta"):
            row = lambda n, other: pl.BlockSpec(
                (share, n), lambda i, pos: (2 * i + (1 - pos[2] if other else pos[2]), 0))
            out = pl.BlockSpec((share, width), lambda i, pos: (i, 0))
            n_exp = exps.shape[1]
            keep, send = call(
                delta_kernel, "delta", (replicas // 2,),
                [row(width, False), row(width, True), row(n_exp, False), row(n_exp, True)],
                [out, out], [jax.ShapeDtypeStruct((rows // 2, width), BF16)] * 2, after=[send],
            )(pos, codes, codes, exps, exps)
            arrived = lax.ppermute(send, "replica", [(i, i ^ 1) for i in range(replicas)])
            pair_sum = call(
                add_kernel, "add", (1,), [part_rows(half, width)] * 2, part_rows(half, width),
                jax.ShapeDtypeStruct((half, width), BF16), after=[w_3, w_1, cot_o],
            )(pos, keep, arrived)
            deltas = lax.all_to_all(
                pair_sum.reshape(replicas // 2, share, width), "replica", 0, 0,
                axis_index_groups=[list(range(k, replicas, 2)) for k in range(2)])
        with jax.named_scope("far"):
            far_up, far_down = call(
                far_grad_kernel, "far_grad", (1,),
                blocks(2, 0) + [part_of((half, width), 0, 0), part_of((half, width), 1, 0)],
                [whole((rows, width))] * 2, [jax.ShapeDtypeStruct((rows, width), BF16)] * 2, after=[pair_sum],
            )(pos, act, act_2, cot, cot_o, w_3, w_1)
            up_o = moved(far_up, up)
            down_o = moved(far_down, down)
        with jax.named_scope("pair_swap"):
            anywhere = pl.BlockSpec(memory_space=pl.ANY)
            send = call(
                lambda *refs: split_kernel(rows, (1, 3, 0), *refs), "split", (1,), [anywhere], anywhere,
                jax.ShapeDtypeStruct((tok, 3 * rows), BF16), after=[far_up], sems=3,
            )(pos, act)
            act_o = moved(send, swap)
        with jax.named_scope("input_grad"):
            shift = lambda x, y, s: (x, y, s - 1)
            flip = lambda x, y, s: (x + 1, y, s - 1)
            out = pl.BlockSpec((tok, rows), lambda i, pos: (0, i))
            own, other = call(
                input_grad_kernel, "input_grad", (NY - 1,),
                [whole((tok, width))] * 2 + [whole((rows, width))] * 3, [out, out],
                [jax.ShapeDtypeStruct((tok, (NY - 1) * rows), BF16)] * 2, after=[send],
            )(pos, cot, cot_o, w, w_1, w_3)
            sent_other, sent_own = moved(other, flip, 1), moved(own, shift, 1)
        with jax.named_scope("outer"):
            cols = width // 2
            wide = pl.BlockSpec((replicas, share, cols), lambda i, pos: (0, 0, i))
            some = pl.BlockSpec((replicas // 2, share, cols), lambda i, pos: (0, 0, i))
            thin = pl.BlockSpec((share, cols), lambda i, pos: (0, i))
            mom_new, mas_new, to_sync = call(
                outer_kernel, "outer", (2,), [some, thin, thin], [thin, thin, wide],
                [jax.ShapeDtypeStruct(mom.shape, F32)] * 2
                + [jax.ShapeDtypeStruct((replicas, share, width), BF16)], after=[own],
            )(pos, deltas, mom, mas)
            synced = lax.all_to_all(to_sync, "replica", 0, 0).reshape(rows, width)
        with jax.named_scope("weight_grad"):
            part, near_1 = near(1, 0, up_o, [to_sync])
            part, near_3 = near(3, 1, down_o, [part])
        with jax.named_scope("input_grad"):
            own, other = call(
                far_input_grad_kernel, "far_input_grad", (1,),
                [whole((tok, width))] * 2 + [part_of((half, width), 1, 0)] * 2, [whole((tok, rows))] * 2,
                [jax.ShapeDtypeStruct((tok, rows), BF16)] * 2, after=[part],
            )(pos, cot, cot_o, up_o, down_o)
            sent_other_2, sent_own_2 = moved(other, flip, 1), moved(own, shift, 1)
        with jax.named_scope("assemble"):
            sent = place(sent_own, sent_own_2, False, [own])
        with jax.named_scope("weight_grad"):
            grad = call(
                last_grad_kernel, "last_grad", (1,), blocks(0, 2) + [whole((rows, width))] * 2,
                whole((rows, width)), jax.ShapeDtypeStruct((rows, width), BF16), after=[sent],
            )(pos, act, act_o, cot, cot_o, near_1, near_3)
        with jax.named_scope("assemble"):
            sent = place(sent_other, sent_other_2, True, [grad], sent)
        return (sent[None, None], grad[None, None], mom_new[None], mas_new[None], synced[None])

    placed = (
        P("replica", "section", "dp", None),
        P("replica", "section", "dp", None),
        P("replica", "section", "dp", None),
        P("replica", "section", "dp", None),
        P("replica", "section", "dp", None),
        P("section", ("dp", "replica"), None),
        P("section", ("dp", "replica"), None),
    )
    return jax.shard_map(
        body,
        mesh=mesh,
        in_specs=placed,
        out_specs=(
            P("replica", "section", "dp", None),
            P("replica", "section", "dp", None),
            P("section", ("dp", "replica"), None),
            P("section", ("dp", "replica"), None),
            P("section", "dp", None),
        ),
        check_vma=False,
    )
```

```python
import jax
import jax.numpy as jnp
from jax import lax
from jax.experimental import pallas as pl
from jax.experimental.pallas import tpu as pltpu
from jax.sharding import PartitionSpec as P

NX, NY = 2, 4
BF16, F32 = jnp.bfloat16, jnp.float32
PARAMS = pltpu.CompilerParams(vmem_limit_bytes=48 * 1024 * 1024)


def call(kernel, name, grid, in_specs, out_specs, out_shape, aliases=None, after=(), sems=0):
    inputs, count = len(in_specs), len(after)

    def with_after(pos, *refs):
        kernel(pos, *refs[:inputs], *refs[inputs + count:])

    run = pl.pallas_call(
        with_after,
        grid_spec=pltpu.PrefetchScalarGridSpec(
            num_scalar_prefetch=1, grid=grid, in_specs=list(in_specs) + [pl.BlockSpec(memory_space=pl.ANY)] * count,
            out_specs=out_specs, scratch_shapes=[pltpu.SemaphoreType.DMA((sems,))] if sems else []),
        out_shape=out_shape,
        input_output_aliases=aliases or {},
        compiler_params=PARAMS,
        cost_estimate=pl.CostEstimate(flops=1, bytes_accessed=1, transcendentals=0),
        name=name,
    )
    return lambda *operands: run(*operands, *after)


def block_of(pos, r):
    return lax.rem(pos[1] + r, NY)


def scaled(codes_ref, exps_ref, out_ref):
    scales = jnp.exp2(exps_ref[...].astype(F32))
    blocks = scales.shape[1]
    wide = codes_ref.shape[1] // blocks
    for b in range(blocks):
        cols = slice(b * wide, (b + 1) * wide)
        out_ref[:, cols] = (codes_ref[:, cols].astype(F32) * scales[:, b:b + 1]).astype(BF16)


def delta_kernel(pos, codes_keep, codes_send, exps_keep, exps_send, keep_ref, send_ref):
    scaled(codes_keep, exps_keep, keep_ref)
    scaled(codes_send, exps_send, send_ref)


def add_kernel(pos, keep, arrived, out_ref):
    out_ref[...] = (keep[...].astype(F32) + arrived[...].astype(F32)).astype(BF16)


def input_grad(c_ref, c_o_ref, w_ref):
    both = jnp.concatenate([c_ref[...], c_o_ref[...]], 0)
    out = lax.dot_general(
        both, w_ref[...], (((1,), (1,)), ((), ())), preferred_element_type=F32).astype(BF16)
    return out[:c_ref.shape[0]], out[c_ref.shape[0]:]


def input_grad_kernel(pos, c_ref, c_o_ref, *refs):
    *w_refs, own_ref, other_ref = refs
    for i, w_ref in enumerate(w_refs):
        @pl.when(pl.program_id(0) == i)
        def _():
            own_ref[...], other_ref[...] = input_grad(c_ref, c_o_ref, w_ref)


def far_input_grad_kernel(pos, c_ref, c_o_ref, up_ref, down_ref, own_ref, other_ref):
    half = up_ref.shape[0]
    own_ref[:, :half], other_ref[:, :half] = input_grad(c_ref, c_o_ref, up_ref)
    own_ref[:, half:], other_ref[:, half:] = input_grad(c_ref, c_o_ref, down_ref)


def partial_grad(a_ref, a_o_ref, c_ref, c_o_ref):
    dims = (((0,), (0,)), ((), ()))
    return lax.dot_general(a_ref[...], c_ref[...], dims, preferred_element_type=F32) + lax.dot_general(
        a_o_ref[...], c_o_ref[...], dims, preferred_element_type=F32)


def far_grad_kernel(pos, a_ref, a_o_ref, c_ref, c_o_ref, w_up, w_down, up_ref, down_ref):
    total = partial_grad(a_ref, a_o_ref, c_ref, c_o_ref).astype(BF16)
    half = total.shape[0] // 2
    up_ref[:half] = total[:half]
    up_ref[half:] = w_up[...]
    down_ref[:half] = total[half:]
    down_ref[half:] = w_down[...]


def near_grad_kernel(upper, pos, a_ref, a_o_ref, c_ref, c_o_ref, arrived, out_ref):
    total = partial_grad(a_ref, a_o_ref, c_ref, c_o_ref)
    half = arrived.shape[0]
    first, second = total[:half], total[half:]
    if upper:
        first = first + arrived[...].astype(F32)
    else:
        second = second + arrived[...].astype(F32)
    out_ref[:half] = first.astype(BF16)
    out_ref[half:] = second.astype(BF16)


def last_grad_kernel(pos, a_ref, a_o_ref, c_ref, c_o_ref, p1, p3, out_ref):
    total = partial_grad(a_ref, a_o_ref, c_ref, c_o_ref)
    total = total + p1[...].astype(F32) + p3[...].astype(F32)
    out_ref[...] = total.astype(BF16)


def outer_kernel(pos, d_ref, mom_ref, mas_ref, mom_out, mas_out, sync_out):
    count = d_ref.shape[0]
    total = d_ref[0].astype(F32)
    for i in range(1, count):
        total = total + d_ref[i].astype(F32)
    mean = total / (2 * count)
    mom = 0.9 * mom_ref[...] + mean
    mas = mas_ref[...] - 0.7 * (mean + 0.9 * mom)
    mom_out[...] = mom
    mas_out[...] = mas
    synced = mas.astype(BF16)
    for i in range(sync_out.shape[0]):
        sync_out[i] = synced


def place_kernel(pos, most, rest, *refs):
    step = pl.program_id(0)
    out_ref = refs[-1]

    @pl.when(step < NY - 1)
    def _():
        out_ref[...] = most[...]

    @pl.when(step == NY - 1)
    def _():
        out_ref[...] = rest[...]


def split_kernel(rows, numbers, pos, a_ref, out_ref, sems):
    first = (1 - pos[0]) * NY
    moves = []
    for k, r in enumerate(numbers):
        at = pl.multiple_of((first + block_of(pos, r)) * rows, rows)
        moves.append(pltpu.make_async_copy(
            a_ref.at[:, pl.ds(at, rows)], out_ref.at[:, pl.ds(k * rows, rows)], sems.at[k]))
    for move in moves:
        move.start()
    for move in moves:
        move.wait()


def copy_kernel(pos, part_ref, *refs):
    refs[-1][...] = part_ref[...]


def solution(mesh):
    sections = mesh.shape["section"]
    replicas = mesh.shape["replica"]

    def moved(value, to, first=0):
        pairs = []
        for x in range(NX):
            for y in range(NY):
                for s in range(first, sections):
                    tx, ty, ts = to(x, y, s)
                    if 0 <= ts < sections:
                        source = (x * NY + y) * sections + s
                        target = (tx % NX * NY + ty % NY) * sections + ts
                        pairs.append((source, target))
        return lax.ppermute(value, ("dp", "section"), pairs)

    def body(act, cot, w, codes, exps, mom, mas):
        act, cot, w, codes, exps, mom, mas = (
            act[0, 0], cot[0, 0], w[0, 0], codes[0, 0], exps[0, 0], mom[0], mas[0])
        rows, width = w.shape
        tok = act.shape[0]
        dp = lax.axis_index("dp")
        pos = jnp.stack([dp // NY, dp % NY, lax.axis_index("replica") % 2]).astype(jnp.int32)
        whole = lambda shape: pl.BlockSpec(shape, lambda *_: (0,) * len(shape))
        share, half = rows // replicas, rows // 2
        up = lambda x, y, s: (x, y + 1, s)
        down = lambda x, y, s: (x, y - 1, s)
        swap = lambda x, y, s: (x + 1, y, s)

        def swapped_blocks(rs, after):
            number, count = rs
            at = lambda i, pos: (0, (1 - pos[0]) * NY + block_of(pos, number(i)))
            send = call(
                copy_kernel, "split", (count,), [pl.BlockSpec((tok, rows), at)],
                pl.BlockSpec((tok, rows), lambda i, pos: (0, i)),
                jax.ShapeDtypeStruct((tok, count * rows), BF16), after=after,
            )(pos, act)
            return send, moved(send, swap)

        def part_rows(n, m):
            return pl.BlockSpec((n, m), lambda i, pos: (i, 0))

        def part_of(shape, i, j):
            return pl.BlockSpec(shape, lambda *_: (i, j))

        def blocks(r, part):
            return [pl.BlockSpec((tok, rows), lambda _, pos: (0, pos[0] * NY + block_of(pos, r))),
                    part_of((tok, rows), 0, part), whole((tok, width)), whole((tok, width))]

        def near(r, part, arrived, after):
            part = call(
                lambda *refs: near_grad_kernel(r == 1, *refs), "near_grad", (1,),
                blocks(r, part) + [part_of((half, width), 0, 0)], whole((rows, width)),
                jax.ShapeDtypeStruct((rows, width), BF16), after=after,
            )(pos, act, act_o, cot, cot_o, arrived)
            return part, moved(part, up if r == 1 else down)

        def place(parts, flip, numbers, after, base=None):
            number = lambda i: numbers[0] if len(numbers) == 1 else i + i // 2 - i // 3 * 2
            at = lambda i, pos: (0, (1 - pos[0] if flip else pos[0]) * NY + block_of(pos, number(i)))
            specs = [pl.BlockSpec((tok, rows), lambda i, pos: (0, jnp.minimum(i, NY - 2))), whole((tok, rows))]
            return call(
                place_kernel if len(parts) == 2 else copy_kernel, "place", (len(numbers),),
                specs[:len(parts)] + ([pl.BlockSpec(memory_space=pl.ANY)] if base is not None else []),
                pl.BlockSpec((tok, rows), at), jax.ShapeDtypeStruct(act.shape, BF16),
                {len(parts) + 1: 0} if base is not None else None, after=after,
            )(pos, *parts, *([base] if base is not None else []))

        with jax.named_scope("pair_swap"):
            send, act_2 = swapped_blocks((lambda i: 2, 1), [])
            cot_o = moved(cot, swap)
        with jax.named_scope("gather_weight"):
            w_3 = moved(w, up)
            w_1 = moved(w, down)
        with jax.named_scope("delta"):
            row = lambda n, other: pl.BlockSpec(
                (share, n), lambda i, pos: (2 * i + (1 - pos[2] if other else pos[2]), 0))
            out = pl.BlockSpec((share, width), lambda i, pos: (i, 0))
            n_exp = exps.shape[1]
            keep, send = call(
                delta_kernel, "delta", (replicas // 2,),
                [row(width, False), row(width, True), row(n_exp, False), row(n_exp, True)],
                [out, out], [jax.ShapeDtypeStruct((rows // 2, width), BF16)] * 2, after=[send],
            )(pos, codes, codes, exps, exps)
            arrived = lax.ppermute(send, "replica", [(i, i ^ 1) for i in range(replicas)])
            pair_sum = call(
                add_kernel, "add", (1,), [part_rows(half, width)] * 2, part_rows(half, width),
                jax.ShapeDtypeStruct((half, width), BF16), after=[w_3, w_1, cot_o],
            )(pos, keep, arrived)
            deltas = lax.all_to_all(
                pair_sum.reshape(replicas // 2, share, width), "replica", 0, 0,
                axis_index_groups=[list(range(k, replicas, 2)) for k in range(2)])
        with jax.named_scope("far"):
            far_up, far_down = call(
                far_grad_kernel, "far_grad", (1,),
                blocks(2, 0) + [part_of((half, width), 0, 0), part_of((half, width), 1, 0)],
                [whole((rows, width))] * 2, [jax.ShapeDtypeStruct((rows, width), BF16)] * 2, after=[pair_sum],
            )(pos, act, act_2, cot, cot_o, w_3, w_1)
            up_o = moved(far_up, up)
            down_o = moved(far_down, down)
        with jax.named_scope("pair_swap"):
            anywhere = pl.BlockSpec(memory_space=pl.ANY)
            send = call(
                lambda *refs: split_kernel(rows, (1, 3, 0), *refs), "split", (1,), [anywhere], anywhere,
                jax.ShapeDtypeStruct((tok, 3 * rows), BF16), after=[far_up], sems=3,
            )(pos, act)
            act_o = moved(send, swap)
        with jax.named_scope("input_grad"):
            shift = lambda x, y, s: (x, y, s - 1)
            flip = lambda x, y, s: (x + 1, y, s - 1)
            out = pl.BlockSpec((tok, rows), lambda i, pos: (0, i))
            own, other = call(
                input_grad_kernel, "input_grad", (NY - 1,),
                [whole((tok, width))] * 2 + [whole((rows, width))] * 3, [out, out],
                [jax.ShapeDtypeStruct((tok, (NY - 1) * rows), BF16)] * 2, after=[send],
            )(pos, cot, cot_o, w, w_1, w_3)
            sent_other, sent_own = moved(other, flip, 1), moved(own, shift, 1)
        with jax.named_scope("outer"):
            cols = width // 2
            wide = pl.BlockSpec((replicas, share, cols), lambda i, pos: (0, 0, i))
            some = pl.BlockSpec((replicas // 2, share, cols), lambda i, pos: (0, 0, i))
            thin = pl.BlockSpec((share, cols), lambda i, pos: (0, i))
            mom_new, mas_new, to_sync = call(
                outer_kernel, "outer", (2,), [some, thin, thin], [thin, thin, wide],
                [jax.ShapeDtypeStruct(mom.shape, F32)] * 2
                + [jax.ShapeDtypeStruct((replicas, share, width), BF16)], after=[own],
            )(pos, deltas, mom, mas)
            synced = lax.all_to_all(to_sync, "replica", 0, 0).reshape(rows, width)
        with jax.named_scope("weight_grad"):
            part, near_1 = near(1, 0, up_o, [to_sync])
            part, near_3 = near(3, 1, down_o, [part])
        with jax.named_scope("input_grad"):
            own, other = call(
                far_input_grad_kernel, "far_input_grad", (1,),
                [whole((tok, width))] * 2 + [part_of((half, width), 1, 0)] * 2, [whole((tok, rows))] * 2,
                [jax.ShapeDtypeStruct((tok, rows), BF16)] * 2, after=[part],
            )(pos, cot, cot_o, up_o, down_o)
            sent_other_2, sent_own_2 = moved(other, flip, 1), moved(own, shift, 1)
        with jax.named_scope("assemble"):
            sent = place([sent_other], True, (0, 1, 3), [own])
        with jax.named_scope("weight_grad"):
            grad = call(
                last_grad_kernel, "last_grad", (1,), blocks(0, 2) + [whole((rows, width))] * 2,
                whole((rows, width)), jax.ShapeDtypeStruct((rows, width), BF16), after=[sent],
            )(pos, act, act_o, cot, cot_o, near_1, near_3)
        with jax.named_scope("assemble"):
            sent = place([sent_own, sent_own_2], False, (0, 1, 3, 2), [grad], sent)
            sent = place([sent_other_2], True, (2,), [], sent)
        return (sent[None, None], grad[None, None], mom_new[None], mas_new[None], synced[None])

    placed = (
        P("replica", "section", "dp", None),
        P("replica", "section", "dp", None),
        P("replica", "section", "dp", None),
        P("replica", "section", "dp", None),
        P("replica", "section", "dp", None),
        P("section", ("dp", "replica"), None),
        P("section", ("dp", "replica"), None),
    )
    return jax.shard_map(
        body,
        mesh=mesh,
        in_specs=placed,
        out_specs=(
            P("replica", "section", "dp", None),
            P("replica", "section", "dp", None),
            P("section", ("dp", "replica"), None),
            P("section", ("dp", "replica"), None),
            P("section", "dp", None),
        ),
        check_vma=False,
    )
```
